128 devices in a mesh: leaf: 32 (over z, x, core), rhs: 4 (over y).
Axes of the slice: x: 4, y: 4, z: 4, core: 2. Of those that a mesh axis runs over, the one named last changes fastest.
Arguments:
- right_sides: float32 [128, 1024, 2048], P('leaf', 'rhs'), may hold values from -6 to 6
- leaf_bases: bfloat16 [128, 1024, 256], P('leaf', 'rhs'), may hold values from -0.1875 to 0.1875
- leaf_expand: bfloat16 [128, 1024, 256], P('leaf', 'rhs'), may hold values from -0.375 to 0.375
- transfer: bfloat16 [8, 128, 2, 256, 256], P(None, 'leaf'), may hold values from -0.375 to 0.375
- skeleton_ranks: int32 [9, 128], P(None, 'leaf'), may hold values from 32 to 256, as said below
- owner_map: int32 [128], replicated, may hold values from 0 to 127, as said below
Outputs:
- product: bfloat16 [128, 1024, 2048], P('leaf', 'rhs')
The draws below stay inside these ranges and needn't reach their ends.
Inputs may be any that keep to these rules, and one draw needn't show every extreme that they name: `skeleton_ranks`: each section has a block of rank 256 and a block of rank 256 // 8. `owner_map`: A permutation of the 128 blocks; the 4 blocks of one index of leaf go to 4 different indices of leaf.
All inputs are finite; a program needn't handle non-finite values.
Results may differ from the reference program's by a relative error of at most 0.017.
Values may be sent and summed in bfloat16 or wider, within the bound.
A program may use at most 128 MiB of HBM per device.

```python
import jax
import jax.numpy as jnp
from jax import lax

POINTS = 1024
RANK = 256
LEAF_DEV = 4
SPLIT_LEVELS = 4
LEVELS = 8
LEAVES = 128
NRHS = 2048
N_LEAF = 32


def draw_skeleton_ranks(key, part):
    section_count = LEVELS + 1
    values = jax.random.randint(jax.random.fold_in(key, 11), (section_count, LEAVES), RANK // 8, RANK + 1)
    chosen = jax.random.randint(jax.random.fold_in(key, 12), (section_count, 1), 0, LEAVES)
    offset = jax.random.randint(jax.random.fold_in(key, 13), (section_count, 1), 1, max(LEAVES, 2))
    chosen_low = (chosen + offset) % LEAVES
    block_ids = jnp.arange(LEAVES)[None, :]
    values = jnp.where(block_ids == chosen_low, RANK // 8, values)
    values = jnp.where(block_ids == chosen, RANK, values)
    return values.astype(jnp.int32)


def shuffle_slots(slot_key):
    return jax.random.permutation(slot_key, LEAF_DEV)


def draw_owner_map(key, part):
    leaf_count = LEAVES // LEAF_DEV
    outer = jax.random.permutation(jax.random.fold_in(key, 21), leaf_count)
    inner = jax.random.permutation(jax.random.fold_in(key, 22), leaf_count)
    offsets = jax.random.permutation(jax.random.fold_in(key, 23), leaf_count)[:LEAF_DEV]
    slot_keys = jax.random.split(jax.random.fold_in(key, 24), leaf_count)
    slot_orders = jax.vmap(shuffle_slots)(slot_keys)
    block_ids = jnp.arange(LEAVES)
    source_dev = block_ids // LEAF_DEV
    source_slot = block_ids % LEAF_DEV
    target = outer[(inner[source_dev] + offsets[source_slot]) % leaf_count]
    return (target * LEAF_DEV + slot_orders[target, source_slot]).astype(jnp.int32)


def block_levels(own_key, dims, cuts, least, high):
    def one(axis_at, blocks):
        steps = jax.random.uniform(jax.random.fold_in(jax.random.fold_in(own_key, 6), axis_at), (blocks,), jnp.float32, least / len(cuts), high / len(cuts))
        return jnp.repeat(jnp.exp(steps), dims[axis_at] // blocks).reshape((-1,) + (1,) * (len(dims) - axis_at - 1))

    factor_of = one(*cuts[0])
    for cut in cuts[1:]:
        factor_of = factor_of * one(*cut)
    return factor_of


def centred(own_key, shape, scale, bound, cuts=(), kind=jnp.bfloat16):
    result = jax.random.normal(own_key, shape, jnp.float32) * scale
    if len(cuts) > 0:
        result = block_levels(own_key, shape, cuts, -0.22, 0.18) * result
    return jnp.clip(result, min=-bound, max=bound).astype(kind)


def setup_inputs(seed: int = 0) -> dict:
    arg_keys = jax.random.split(jax.random.key(seed), 7)
    right_sides = centred(arg_keys[0], (LEAVES, POINTS, NRHS), 1.0, 6.0, ((0, 32), (1, 4)), jnp.float32)
    leaf_bases = centred(arg_keys[1], (LEAVES, POINTS, RANK), POINTS ** -0.5, 0.1875, ((0, 32), (1, 4)))
    leaf_expand = centred(arg_keys[2], (LEAVES, POINTS, RANK), RANK ** -0.5, 0.375, ((0, 32), (1, 4)))
    transfer = centred(arg_keys[3], (LEVELS, LEAVES, 2, RANK, RANK), RANK ** -0.5, 0.375, ((1, 32),))
    skeleton_ranks = draw_skeleton_ranks(jax.random.fold_in(arg_keys[6], 71), 0)
    owner_map = draw_owner_map(jax.random.fold_in(arg_keys[6], 71), 0)
    return {"right_sides": right_sides, "leaf_bases": leaf_bases, "leaf_expand": leaf_expand, "transfer": transfer, "skeleton_ranks": skeleton_ranks, "owner_map": owner_map}


def rank_mask(values, rank_row):
    row_ids = lax.broadcasted_iota(jnp.int32, values.shape, 1)
    return jnp.where(row_ids < rank_row[:, None, None], values, jnp.float32(0.0))


def project_one(pair):
    return jnp.dot(pair[0].T, pair[1], preferred_element_type=jnp.float32)


def combine_one(group):
    own_term = jnp.dot(group[0], group[2], preferred_element_type=jnp.float32)
    far_term = jnp.dot(group[1], group[3], preferred_element_type=jnp.float32)
    return own_term + far_term


def expand_one(pair):
    return jnp.dot(pair[0], pair[1], preferred_element_type=jnp.float32).astype(jnp.bfloat16)


def reference(right_sides, leaf_bases, leaf_expand, transfer, skeleton_ranks, owner_map):
    rounded = right_sides.astype(jnp.bfloat16)
    projected = lax.map(project_one, (leaf_bases, rounded))
    skeleton = rank_mask(projected, skeleton_ranks[0]).astype(jnp.bfloat16)
    log_width = N_LEAF.bit_length() - 1
    block_ids = jnp.arange(LEAVES, dtype=jnp.int32)
    for level in range(LEVELS):
        if level == SPLIT_LEVELS:
            skeleton = jnp.zeros_like(skeleton).at[owner_map].set(skeleton)
        bit_index = level % log_width
        partner_ids = jnp.bitwise_xor(block_ids, jnp.int32(LEAF_DEV << bit_index))
        partner = skeleton[partner_ids]
        summed = lax.map(combine_one, (transfer[level, :, 0], transfer[level, :, 1], skeleton, partner))
        skeleton = rank_mask(summed, skeleton_ranks[level + 1]).astype(jnp.bfloat16)
    return lax.map(expand_one, (leaf_expand, skeleton))
```

```python
import functools

import jax
import jax.numpy as jnp
import numpy as np
from jax import lax
from jax.experimental import pallas as pl
from jax.experimental.pallas import tpu as pltpu
from jax.sharding import PartitionSpec as P

MESH = pl.DeviceIdType.MESH
BF16 = jnp.bfloat16
F32 = jnp.float32

RANK = 256
HALF = RANK // 2
SIDE = 4
CHUNKS = 4
PART = 128
WIDE = SIDE * PART
PIECE = RANK // (SIDE * SIDE)
STAGES = 14
LEVELS = 8


def dot(a, b):
    return jnp.dot(a, b, preferred_element_type=F32)


def butterfly(
    sides, bases, transfer, ranks, moves, out,
    xin, raw, bt, pbuf, rel, direct, fin, acc,
    s0, p0, s1p, s1q, s3, p3, s4, spread, perm, packed, s4m, p4, s5, p5, s8q, s8p, tq,
    in_sem, base_sem, t_sem, tx_send, tx_recv,
    rs_send, rs_recv, core_send, core_recv, x_send, x_recv, z_send, z_recv,
    sw_send, sw_recv, ag_send, ag_recv,
):
    leaf = lax.axis_index("leaf")
    y = lax.axis_index("rhs")
    c = lax.rem(leaf, 2)
    x = lax.rem(lax.div(leaf, 2), SIDE)
    z = lax.div(leaf, 2 * SIDE)
    zy = z * SIDE + y

    def device(z_at, x_at, c_at, y_at):
        return {"leaf": z_at * (2 * SIDE) + x_at * 2 + c_at, "rhs": y_at}

    def turn(at, by):
        return lax.rem(at + by, SIDE)

    def remote(src, dst, send, recv, to):
        return pltpu.make_async_remote_copy(
            src_ref=src, dst_ref=dst, send_sem=send, recv_sem=recv, device_id=to, device_id_type=MESH
        )

    up, down = device(z, x, c, turn(y, 1)), device(z, x, c, turn(y, 3))
    twin = device(z, x, 1 - c, y)
    z_near = device(z + 1 - 2 * lax.rem(z, 2), x, c, y)
    z_far = device(turn(z, 2), x, c, y)
    x_right, x_left = device(z, turn(x, 1), c, y), device(z, turn(x, 3), c, y)

    def plane(by):
        at = lax.rem(zy + by, SIDE * SIDE)
        return at, device(lax.div(at, SIDE), x, c, lax.rem(at, SIDE))

    barrier = pltpu.get_barrier_semaphore()
    for by in range(1, SIDE * SIDE):
        pl.semaphore_signal(barrier, inc=1, device_id=plane(by)[1], device_id_type=MESH)
    for by in range(1, SIDE):
        pl.semaphore_signal(barrier, inc=1, device_id=device(z, turn(x, by), c, y), device_id_type=MESH)
    pl.semaphore_signal(barrier, inc=1, device_id=twin, device_id_type=MESH)

    def load_sides(k):
        return pltpu.make_async_copy(
            sides.at[:, :, pl.ds(pl.multiple_of(k * WIDE, WIDE), WIDE)], xin.at[k], in_sem.at[k]
        )

    def load_transfer(level):
        return pltpu.make_async_copy(transfer.at[level, y], tq.at[level, x], t_sem.at[level])

    load_bases = pltpu.make_async_copy(bases, raw, base_sem)
    load_bases.start()
    load_sides(0).start()
    for level in range(LEVELS):
        load_transfer(level).start()
    for k in range(1, CHUNKS):
        load_sides(k).start()

    load_bases.wait()
    rows = lax.broadcasted_iota(jnp.int32, (RANK, RANK), 0)
    for j in range(SIDE):
        flipped = raw[j].astype(F32).T
        bt[j] = jnp.where(rows < ranks[0, j], flipped, 0.0).astype(BF16)

    def t_right(level):
        return remote(tq.at[level, x], tq.at[level, x], tx_send.at[level, 0], tx_recv.at[level, 0], x_right)

    def t_left(level):
        return remote(tq.at[level, x], tq.at[level, x], tx_send.at[level, 1], tx_recv.at[level, 1], x_left)

    def t_on_right(level):
        part = tq.at[level, turn(x, 3), 0]
        return remote(part, part, tx_send.at[level, 2], tx_recv.at[level, 2], x_right)

    def t_on_left(level):
        part = tq.at[level, turn(x, 1), 1]
        return remote(part, part, tx_send.at[level, 3], tx_recv.at[level, 3], x_left)

    def t_ready(level):
        load_transfer(level).wait()
        keep = rows < ranks[level + 1, y]
        for side in range(2):
            tq[level, x, side] = jnp.where(keep, tq[level, x, side].astype(F32), 0.0).astype(BF16)

    def t_begin(level):
        t_ready(level)
        t_right(level).start()
        t_left(level).start()

    def t_forward(level):
        t_right(level).wait()
        t_left(level).wait()
        t_on_right(level).start()
        t_on_left(level).start()

    def t_end(level):
        t_on_right(level).wait()
        t_on_left(level).wait()

    low, high = pl.ds(0, HALF), pl.ds(HALF, HALF)

    def sum_copies(k):
        across, above, below = turn(y, 2), turn(y, 1), turn(y, 3)
        first = [
            remote(pbuf.at[k, across, low], rel.at[k, 0], rs_send.at[k, 0], rs_recv.at[k, 0], down),
            remote(pbuf.at[k, across, high], rel.at[k, 1], rs_send.at[k, 1], rs_recv.at[k, 1], up),
        ]
        near_up = remote(pbuf.at[k, above, low], direct.at[k, 0], rs_send.at[k, 2], rs_recv.at[k, 2], up)
        near_down = remote(pbuf.at[k, below, high], direct.at[k, 1], rs_send.at[k, 3], rs_recv.at[k, 3], down)
        second = [
            remote(acc.at[k, 0], fin.at[k, 0], rs_send.at[k, 4], rs_recv.at[k, 4], down),
            remote(acc.at[k, 1], fin.at[k, 1], rs_send.at[k, 5], rs_recv.at[k, 5], up),
        ]
        return first, near_up, near_down, second

    def core_copy(k, n, src, dst):
        return remote(src, dst, core_send.at[k, n], core_recv.at[k, n], twin)

    def x_copies(k, n, src, dst):
        copies = [pltpu.make_async_copy(src.at[k, x], dst.at[k, x], x_recv.at[k, n, 0])]
        for by in range(1, SIDE):
            to = turn(x, by)
            copies.append(
                remote(src.at[k, to], dst.at[k, x], x_send.at[k, n, by], x_recv.at[k, n, by], device(z, to, c, y))
            )
        return copies

    def z_copy(k, n, src, dst, to):
        return remote(src.at[k], dst.at[k], z_send.at[k, n], z_recv.at[k, n], to)

    def piece(at):
        return pl.ds(pl.multiple_of(at * PIECE, PIECE), PIECE)

    def group(at):
        return pl.ds(at * SIDE, SIDE)

    mine = pl.ds(c * (SIDE**3), SIDE**3)

    def spread_start(k):
        land = pl.ds(c * (SIDE**3) + zy * SIDE, SIDE)
        pltpu.make_async_copy(s4.at[k, :, piece(zy)], spread.at[k, land], sw_recv.at[k, 0]).start()
        for by in range(1, SIDE * SIDE):
            at, to = plane(by)
            remote(
                s4.at[k, :, piece(at)], spread.at[k, land], sw_send.at[k, 0], sw_recv.at[k, 0], to
            ).start()

    def spread_wait(k):
        whole = spread.at[k, mine]
        pltpu.make_async_copy(whole, whole, sw_recv.at[k, 0]).wait()
        sent = spread.at[k, pl.ds(0, SIDE**3 - SIDE)]
        pltpu.make_async_copy(sent, sent, sw_send.at[k, 0]).wait()

    def gather_start(k):
        land = piece(zy)
        pltpu.make_async_copy(packed.at[k, group(zy)], s4m.at[k, :, land], sw_recv.at[k, 1]).start()
        for by in range(1, SIDE * SIDE):
            at, to = plane(by)
            remote(
                packed.at[k, group(at)], s4m.at[k, :, land], sw_send.at[k, 1], sw_recv.at[k, 1], to
            ).start()

    def gather_wait(k):
        whole = s4m.at[k]
        pltpu.make_async_copy(whole, whole, sw_recv.at[k, 1]).wait()
        sent = packed.at[k, pl.ds(0, SIDE**3 - SIDE)]
        pltpu.make_async_copy(sent, sent, sw_send.at[k, 1]).wait()

    def columns_of(k):
        return pl.ds(k * SIDE, SIDE)

    def all_copies(k):
        src, dst = s8p.at[k], out.at[y, columns_of(k)]
        keep = pltpu.make_async_copy(src, dst, ag_recv.at[k, 4])
        first = [
            remote(src, dst, ag_send.at[k, 0], ag_recv.at[k, 0], up),
            remote(src, dst, ag_send.at[k, 1], ag_recv.at[k, 1], down),
        ]
        from_down = out.at[turn(y, 3), columns_of(k), low]
        from_up = out.at[turn(y, 1), columns_of(k), high]
        second = [
            remote(from_down, from_down, ag_send.at[k, 2], ag_recv.at[k, 2], up),
            remote(from_up, from_up, ag_send.at[k, 3], ag_recv.at[k, 3], down),
        ]
        return keep, first, second

    def level_of(level, near, far):
        return [
            (dot(tq[level, i, 0], near[i]) + dot(tq[level, i, 1], far[i])).astype(BF16) for i in range(SIDE)
        ]

    def project(k):
        load_sides(k).wait()
        first, near_up, near_down, _ = sum_copies(k)
        for by, copies in ((2, first), (1, [near_up]), (3, [near_down]), (0, [])):
            j = turn(y, by)
            pbuf[k, j] = dot(bt[j], xin[k, j].astype(BF16)).astype(BF16)
            for copy in copies:
                copy.start()

    def relay(k):
        first, _, _, second = sum_copies(k)
        first[0].wait()
        acc[k, 0] = (rel[k, 0].astype(F32) + pbuf[k, turn(y, 3), :HALF].astype(F32)).astype(BF16)
        second[0].start()
        first[1].wait()
        acc[k, 1] = (rel[k, 1].astype(F32) + pbuf[k, turn(y, 1), HALF:].astype(F32)).astype(BF16)
        second[1].start()

    def total(k):
        _, near_up, near_down, second = sum_copies(k)
        for copy in (near_up, near_down, *second):
            copy.wait()
        for half in range(2):
            at = pl.ds(half * HALF, HALF)
            s0[k, at] = (
                pbuf[k, y, at].astype(F32) + direct[k, half].astype(F32) + fin[k, half].astype(F32)
            ).astype(BF16)
        core_copy(k, 0, s0.at[k], p0.at[k]).start()

    def level_0(k):
        core_copy(k, 0, s0.at[k], p0.at[k]).wait()
        done = (dot(tq[0, x, 0], s0[k]) + dot(tq[0, x, 1], p0[k])).astype(BF16)
        for part in range(SIDE):
            s1p[k, part] = done[:, part * PART : (part + 1) * PART]
        for copy in x_copies(k, 0, s1p, s1q):
            copy.start()

    def levels_1_2(k):
        @pl.when(k == 0)
        def _():
            t_end(1)
            t_end(2)

        for copy in x_copies(k, 0, s1p, s1q):
            copy.wait()
        now = [s1q[k, i] for i in range(SIDE)]
        now = level_of(1, now, [now[i ^ 1] for i in range(SIDE)])
        now = level_of(2, now, [now[i ^ 2] for i in range(SIDE)])
        for i in range(SIDE):
            s3[k, i] = now[i]
        z_copy(k, 0, s3, p3, z_near).start()

    def level_3(k):
        @pl.when(k == 0)
        def _():
            t_end(3)

        z_copy(k, 0, s3, p3, z_near).wait()
        now = level_of(3, [s3[k, i] for i in range(SIDE)], [p3[k, i] for i in range(SIDE)])
        for i in range(SIDE):
            s4[k, i] = now[i]
        spread_start(k)

    def share(k):
        spread_wait(k)
        core_copy(k, 1, spread.at[k, mine], spread.at[k, mine]).start()

    def switch(k):
        core_copy(k, 1, spread.at[k, mine], spread.at[k, mine]).wait()
        for b in range(2 * SIDE**3):
            perm[b] = spread[k, b]
        base = c * (SIDE**3)
        for i in range(SIDE**3):
            packed[k, i] = perm[moves[base + i]]
        gather_start(k)

    def pass_far(k):
        gather_wait(k)
        z_copy(k, 1, s4m, p4, z_far).start()

    def level_4(k):
        @pl.when(k == 0)
        def _():
            t_end(4)

        z_copy(k, 1, s4m, p4, z_far).wait()
        now = level_of(4, [s4m[k, i] for i in range(SIDE)], [p4[k, i] for i in range(SIDE)])
        for i in range(SIDE):
            s5[k, i] = now[i]
        core_copy(k, 2, s5.at[k], p5.at[k]).start()

    def levels_5_7(k):
        @pl.when(k == 0)
        def _():
            for level in (5, 6, 7):
                t_end(level)

        core_copy(k, 2, s5.at[k], p5.at[k]).wait()
        now = level_of(5, [s5[k, i] for i in range(SIDE)], [p5[k, i] for i in range(SIDE)])
        now = level_of(6, now, [now[i ^ 1] for i in range(SIDE)])
        now = level_of(7, now, [now[i ^ 2] for i in range(SIDE)])
        for i in range(SIDE):
            s8q[k, i] = now[i]
        for copy in x_copies(k, 1, s8q, s8p):
            copy.start()

    def give(k):
        for copy in x_copies(k, 1, s8q, s8p):
            copy.wait()
        keep, first, _ = all_copies(k)
        for copy in (*first, keep):
            copy.start()

    def give_on(k):
        _, first, second = all_copies(k)
        for copy, onward in zip(first, second):
            copy.wait()
            onward.start()

    def finish(k):
        keep, _, second = all_copies(k)
        for copy in (*second, keep):
            copy.wait()

    stages = [
        project, relay, total, level_0, levels_1_2, level_3, share, switch,
        pass_far, level_4, levels_5_7, give, give_on, finish,
    ]
    order = [0, 1, 2] + list(range(STAGES - 1, 2, -1))

    pl.semaphore_wait(barrier, SIDE * SIDE + SIDE - 1)
    t_begin(1)
    t_ready(0)

    @pl.loop(0, STAGES + CHUNKS - 1)
    def _(t):
        for s in order:
            k = t - s

            @pl.when(jnp.logical_and(k >= 0, k < CHUNKS))
            def _(s=s, k=k):
                stages[s](k)

            if s == 0:

                @pl.when(t < LEVELS - 2)
                def _():
                    t_begin(t + 2)

            if s == 2:

                @pl.when(t < LEVELS - 1)
                def _():
                    t_forward(t + 1)


def gathered(right_sides, leaf_bases, transfer, ranks, moves):
    dma, vmem = pltpu.SemaphoreType.DMA, pltpu.VMEM
    wide = (CHUNKS, RANK, WIDE)
    half = (CHUNKS, 2, HALF, WIDE)
    parts = (CHUNKS, SIDE, RANK, PART)
    blocks = 2 * SIDE**3
    scratch = [
        vmem((CHUNKS, SIDE, RANK, WIDE), F32),
        vmem((SIDE, RANK, RANK), BF16),
        vmem((SIDE, RANK, RANK), BF16),
        vmem((CHUNKS, SIDE, RANK, WIDE), BF16),
        vmem(half, BF16), vmem(half, BF16), vmem(half, BF16), vmem(half, BF16),
        vmem(wide, BF16), vmem(wide, BF16),
        vmem(parts, BF16), vmem(parts, BF16),
        vmem(parts, BF16), vmem(parts, BF16), vmem(parts, BF16),
        vmem((CHUNKS, blocks, PIECE, PART), BF16),
        vmem((blocks, PIECE, PART), BF16),
        vmem((CHUNKS, blocks // 2, PIECE, PART), BF16),
        vmem(parts, BF16), vmem(parts, BF16),
        vmem(parts, BF16), vmem(parts, BF16),
        vmem(parts, BF16), vmem(parts, BF16),
        vmem((LEVELS, SIDE, 2, RANK, RANK), BF16),
        dma((CHUNKS,)), dma(()), dma((LEVELS,)), dma((LEVELS, 4)), dma((LEVELS, 4)),
        dma((CHUNKS, 6)), dma((CHUNKS, 6)), dma((CHUNKS, 3)), dma((CHUNKS, 3)),
        dma((CHUNKS, 2, SIDE)), dma((CHUNKS, 2, SIDE)), dma((CHUNKS, 2)), dma((CHUNKS, 2)),
        dma((CHUNKS, 2)), dma((CHUNKS, 2)), dma((CHUNKS, 4)), dma((CHUNKS, 5)),
    ]
    anywhere = pl.BlockSpec(memory_space=pl.ANY)
    scalars = pl.BlockSpec(memory_space=pltpu.SMEM)
    return pl.pallas_call(
        butterfly,
        out_shape=jax.ShapeDtypeStruct((SIDE, CHUNKS * SIDE, RANK, PART), BF16),
        in_specs=[anywhere, anywhere, anywhere, scalars, scalars],
        out_specs=anywhere,
        scratch_shapes=scratch,
        compiler_params=pltpu.CompilerParams(
            collective_id=0, has_side_effects=True, vmem_limit_bytes=58 * 1024 * 1024
        ),
        cost_estimate=pl.CostEstimate(
            flops=6 * 10**9, bytes_accessed=24 * 2**20, transcendentals=0
        ),
        name="butterfly",
    )(right_sides, leaf_bases, transfer, ranks, moves)


def expand_block(expand, skeleton, product):
    for part in range(skeleton.shape[1]):
        product[0, :, part * PART : (part + 1) * PART] = dot(expand[0], skeleton[0, part]).astype(BF16)


def expanded(leaf_expand, skeleton):
    split = 2
    parts = skeleton.shape[1] // split
    return pl.pallas_call(
        expand_block,
        grid=(SIDE, split),
        out_shape=jax.ShapeDtypeStruct((SIDE, RANK, CHUNKS * WIDE), BF16),
        in_specs=[
            pl.BlockSpec((1, RANK, RANK), lambda j, h: (j, 0, 0)),
            pl.BlockSpec((1, parts, RANK, PART), lambda j, h: (j, h, 0, 0)),
        ],
        out_specs=pl.BlockSpec((1, RANK, parts * PART), lambda j, h: (j, 0, h)),
        compiler_params=pltpu.CompilerParams(vmem_limit_bytes=32 * 1024 * 1024),
        name="expand",
    )(leaf_expand, skeleton)


def switch_table(owner_map):
    place = np.arange(2 * SIDE**3)
    c, zy, x = place // SIDE**3, place // SIDE % (SIDE * SIDE), place % SIDE
    block_at = ((zy // SIDE) * (2 * SIDE) + x * 2 + c) * SIDE + zy % SIDE
    place_of = np.zeros_like(place)
    place_of[block_at] = place
    hit = owner_map[None, :] == jnp.asarray(block_at, jnp.int32)[:, None]
    return jnp.sum(jnp.where(hit, jnp.asarray(place_of, jnp.int32)[None, :], 0), axis=1, dtype=jnp.int32)


def local(right_sides, leaf_bases, leaf_expand, transfer, skeleton_ranks, owner_map):
    skeleton = gathered(right_sides, leaf_bases, transfer, skeleton_ranks, switch_table(owner_map))
    return expanded(leaf_expand, skeleton)


def solution(mesh):
    in_specs = (
        P("leaf", "rhs", None),
        P("leaf", "rhs", None),
        P("leaf", "rhs", None),
        P(None, "leaf", None, None, None),
        P(None, "leaf"),
        P(),
    )
    out_specs = P("leaf", "rhs", None)
    return jax.shard_map(local, mesh=mesh, in_specs=in_specs, out_specs=out_specs, check_vma=False)
```

```python
import functools

import jax
import jax.numpy as jnp
import numpy as np
from jax import lax
from jax.experimental import pallas as pl
from jax.experimental.pallas import tpu as pltpu
from jax.sharding import PartitionSpec as P

MESH = pl.DeviceIdType.MESH
BF16 = jnp.bfloat16
F32 = jnp.float32

RANK = 256
HALF = RANK // 2
SIDE = 4
CHUNKS = 4
PART = 128
WIDE = SIDE * PART
QUARTER = RANK // SIDE
PIECE = QUARTER // SIDE
PLANE = SIDE * SIDE
BLOCKS = SIDE**3
LEVELS = 8
HALFWAY = 3

BEGIN, FORWARD = 14, 15
ORDER = [
    (0, 0), (14, 2), (0, 1), (1, 0), (14, 3), (1, 1), (15, 2), (0, 2), (15, 1), (2, 0),
    (15, 3), (3, 0), (2, 1), (1, 2), (3, 1), (0, 3), (14, 4), (4, 0), (2, 2), (1, 3),
    (3, 2), (14, 6), (4, 1), (2, 3), (5, 0), (3, 3), (14, 7), (4, 2), (5, 1), (6, 0),
    (15, 4), (14, 5), (4, 3), (7, 0), (6, 1), (15, 6), (5, 2), (7, 1), (8, 0), (15, 7),
    (5, 3), (8, 1), (6, 2), (15, 5), (6, 3), (7, 2), (9, 0), (10, 0), (9, 1), (7, 3),
    (8, 2), (10, 1), (11, 0), (8, 3), (11, 1), (9, 2), (12, 0), (10, 2), (9, 3), (12, 1),
    (10, 3), (11, 2), (11, 3), (13, 1), (13, 0), (12, 2), (12, 3), (13, 2), (13, 3),
]


def first_chunk(stage):
    return next(at for event, at in ORDER if event == stage)


def dot(a, b):
    return jnp.dot(a, b, preferred_element_type=F32)


def butterfly(
    sides, bases, transfer, ranks, moves, out,
    xin, raw, bt, pbuf, rel, direct, fin, acc,
    s0, p0, s1p, s1q, terms, met, cut, spread, perm, packed, strips, pairs, s4, s5, p5, s8q, s8p, tq, swap,
    in_sem, base_sem, t_sem, tx_send, tx_recv,
    rs_send, rs_recv, core_send, core_recv, all_send, all_recv, swap_send, swap_recv, ag_send, ag_recv,
):
    leaf = lax.axis_index("leaf")
    y = lax.axis_index("rhs")
    c = lax.rem(leaf, 2)
    x = lax.rem(lax.div(leaf, 2), SIDE)
    z = lax.div(leaf, 2 * SIDE)

    def device(z_at, x_at, c_at, y_at):
        return {"leaf": z_at * (2 * SIDE) + x_at * 2 + c_at, "rhs": y_at}

    def turn(at, by):
        return lax.rem(at + by, SIDE)

    def remote(src, dst, send, recv, to):
        return pltpu.make_async_remote_copy(
            src_ref=src, dst_ref=dst, send_sem=send, recv_sem=recv, device_id=to, device_id_type=MESH
        )

    up, down = device(z, x, c, turn(y, 1)), device(z, x, c, turn(y, 3))
    twin = device(z, x, 1 - c, y)
    z_near = device(z + 1 - 2 * lax.rem(z, 2), x, c, y)
    x_right, x_left = device(z, turn(x, 1), c, y), device(z, turn(x, 3), c, y)

    barrier = pltpu.get_barrier_semaphore()
    for by in range(1, SIDE):
        for peer in (device(turn(z, by), x, c, y), device(z, turn(x, by), c, y), device(z, x, c, turn(y, by))):
            pl.semaphore_signal(barrier, inc=1, device_id=peer, device_id_type=MESH)
    pl.semaphore_signal(barrier, inc=1, device_id=twin, device_id_type=MESH)

    def load_sides(k):
        return pltpu.make_async_copy(
            sides.at[:, :, pl.ds(pl.multiple_of(k * WIDE, WIDE), WIDE)], xin.at[k], in_sem.at[k]
        )

    def load_transfer(level):
        land = swap if level == HALFWAY else tq.at[level, x]
        return pltpu.make_async_copy(transfer.at[level, y], land, t_sem.at[level])

    load_bases = pltpu.make_async_copy(bases, raw, base_sem)
    load_bases.start()
    load_transfer(1).start()
    load_sides(0).start()
    for level in (HALFWAY, 0, 2, 4, 5, 6, 7):
        load_transfer(level).start()
    for k in range(1, CHUNKS):
        load_sides(k).start()

    rows = lax.broadcasted_iota(jnp.int32, (RANK, RANK), 0)

    def flip_bases():
        load_bases.wait()
        for j in range(SIDE):
            flipped = raw[j].astype(F32).T
            bt[j] = jnp.where(rows < ranks[0, j], flipped, 0.0).astype(BF16)

    def t_right(level):
        return remote(tq.at[level, x], tq.at[level, x], tx_send.at[level, 0], tx_recv.at[level, 0], x_right)

    def t_left(level):
        return remote(tq.at[level, x], tq.at[level, x], tx_send.at[level, 1], tx_recv.at[level, 1], x_left)

    def t_on_right(level):
        part = tq.at[level, turn(x, 3), 0]
        return remote(part, part, tx_send.at[level, 2], tx_recv.at[level, 2], x_right)

    def t_on_left(level):
        part = tq.at[level, turn(x, 1), 1]
        return remote(part, part, tx_send.at[level, 3], tx_recv.at[level, 3], x_left)

    def masked(level, matrix):
        return jnp.where(rows < ranks[level + 1, y], matrix.astype(F32), 0.0).astype(BF16)

    def t_ready(level):
        load_transfer(level).wait()
        for side in range(2):
            tq[level, x, side] = masked(level, tq[level, x, side])

    t_swap = remote(swap.at[1], tq.at[HALFWAY, x, 1], swap_send, swap_recv, z_near)

    def t_swap_begin():
        load_transfer(HALFWAY).wait()
        tq[HALFWAY, x, 0] = masked(HALFWAY, swap[0])
        swap[1] = masked(HALFWAY, swap[1])
        t_swap.start()

    def t_begin(level):
        if level == HALFWAY:
            t_swap.wait()
        else:
            t_ready(level)
        t_right(level).start()
        t_left(level).start()

    def t_forward(level):
        t_right(level).wait()
        t_left(level).wait()
        t_on_right(level).start()
        t_on_left(level).start()

    def t_end(level):
        t_on_right(level).wait()
        t_on_left(level).wait()

    low, high = pl.ds(0, HALF), pl.ds(HALF, HALF)

    def sum_copies(k):
        across, above, below = turn(y, 2), turn(y, 1), turn(y, 3)
        first = [
            remote(pbuf.at[k, across, low], rel.at[k, 0], rs_send.at[k, 0], rs_recv.at[k, 0], down),
            remote(pbuf.at[k, across, high], rel.at[k, 1], rs_send.at[k, 1], rs_recv.at[k, 1], up),
        ]
        near_up = remote(pbuf.at[k, above, low], direct.at[k, 0], rs_send.at[k, 2], rs_recv.at[k, 2], up)
        near_down = remote(pbuf.at[k, below, high], direct.at[k, 1], rs_send.at[k, 3], rs_recv.at[k, 3], down)
        second = [
            remote(acc.at[k, 0], fin.at[k, 0], rs_send.at[k, 4], rs_recv.at[k, 4], down),
            remote(acc.at[k, 1], fin.at[k, 1], rs_send.at[k, 5], rs_recv.at[k, 5], up),
        ]
        return first, near_up, near_down, second

    def core_copy(k, n, src, dst):
        return remote(src, dst, core_send.at[k, n], core_recv.at[k, n], twin)

    def every(k, n, src_of, dst, me, device_of):
        copies = [pltpu.make_async_copy(src_of(me), dst, all_recv.at[k, n, 0])]
        for by in range(1, SIDE):
            to = turn(me, by)
            copies.append(remote(src_of(to), dst, all_send.at[k, n, by], all_recv.at[k, n, by], device_of(to)))
        return copies

    def along_x(k, n, src_of, dst):
        return every(k, n, src_of, dst, x, lambda to: device(z, to, c, y))

    def along_y(k, n, src_of, dst):
        return every(k, n, src_of, dst, y, lambda to: device(z, x, c, to))

    def along_z(k, n, src_of, dst):
        return every(k, n, src_of, dst, z, lambda to: device(to, x, c, y))

    def x_in(k):
        return along_x(k, 0, lambda to: s1p.at[k, to], s1q.at[k, x])

    def z_spread(k):
        return along_z(k, 1, lambda to: terms.at[k, to], met.at[k, z])

    def y_spread(k):
        land = spread.at[k, pl.ds(c * BLOCKS + y * PLANE, PLANE)]
        return along_y(k, 2, lambda to: cut.at[k, to], land)

    def y_gather(k):
        return along_y(k, 3, lambda to: packed.at[k, pl.ds(to * PLANE, PLANE)], strips.at[k, y])

    def z_gather(k):
        land = s4.at[k, :, :, pl.ds(pl.multiple_of(z * QUARTER, QUARTER), QUARTER)]
        return along_z(k, 4, lambda to: pairs.at[k, lax.rem(to, 2)], land)

    def x_out(k):
        return along_x(k, 5, lambda to: s8q.at[k, to], s8p.at[k, x])

    mine = pl.ds(c * BLOCKS, BLOCKS)

    def start(copies):
        for copy in copies:
            copy.start()

    def wait(copies):
        for copy in copies:
            copy.wait()

    def columns_of(k):
        return pl.ds(k * SIDE, SIDE)

    def all_copies(k):
        columns = columns_of(k)
        keep = pltpu.make_async_copy(s8p.at[k], out.at[y, columns], ag_recv.at[k, 6])

        def give(n, half, to):
            return remote(
                s8p.at[k, :, half], out.at[y, columns, half], ag_send.at[k, n], ag_recv.at[k, n], to
            )

        def onward(n, at, half, to):
            part = out.at[at, columns, half]
            return remote(part, part, ag_send.at[k, n], ag_recv.at[k, n], to)

        first = [give(0, low, up), give(1, high, down)]
        second = [give(2, high, up), give(3, low, down)]
        third = [onward(4, turn(y, 3), low, up), onward(5, turn(y, 1), high, down)]
        return keep, first, second, third

    def level_of(level, near, far):
        return [
            (dot(tq[level, i, 0], near[i]) + dot(tq[level, i, 1], far[i])).astype(BF16) for i in range(SIDE)
        ]

    def project(k):
        load_sides(k).wait()
        first, near_up, near_down, _ = sum_copies(k)
        for by, copies in ((2, first), (1, [near_up]), (3, [near_down]), (0, [])):
            j = turn(y, by)
            pbuf[k, j] = dot(bt[j], xin[k, j].astype(BF16)).astype(BF16)
            for copy in copies:
                copy.start()

    def relay(k):
        first, _, _, second = sum_copies(k)
        first[0].wait()
        acc[k, 0] = (rel[k, 0].astype(F32) + pbuf[k, turn(y, 3), :HALF].astype(F32)).astype(BF16)
        second[0].start()
        first[1].wait()
        acc[k, 1] = (rel[k, 1].astype(F32) + pbuf[k, turn(y, 1), HALF:].astype(F32)).astype(BF16)
        second[1].start()

    def total(k):
        _, near_up, near_down, second = sum_copies(k)
        for copy in (near_up, near_down, *second):
            copy.wait()
        for half in range(2):
            at = pl.ds(half * HALF, HALF)
            s0[k, at] = (
                pbuf[k, y, at].astype(F32) + direct[k, half].astype(F32) + fin[k, half].astype(F32)
            ).astype(BF16)
        core_copy(k, 0, s0.at[k], p0.at[k]).start()

    def level_0(k):
        core_copy(k, 0, s0.at[k], p0.at[k]).wait()
        done = (dot(tq[0, x, 0], s0[k]) + dot(tq[0, x, 1], p0[k])).astype(BF16)
        for part in range(SIDE):
            s1p[k, part] = done[:, part * PART : (part + 1) * PART]
        start(x_in(k))

    def levels_1_3(k):
        if k == first_chunk(4):
            for level in (1, 2, 3):
                t_end(level)
        wait(x_in(k))
        now = [s1q[k, i] for i in range(SIDE)]
        now = level_of(1, now, [now[i ^ 1] for i in range(SIDE)])
        now = level_of(2, now, [now[i ^ 2] for i in range(SIDE)])
        for i in range(SIDE):
            for side in range(2):
                term = dot(tq[HALFWAY, i, side], now[i]).astype(BF16)
                for part in range(SIDE):
                    terms[k, part, side, i] = term[part * QUARTER : (part + 1) * QUARTER]
        start(z_spread(k))

    def add(k):
        wait(z_spread(k))
        for at in range(SIDE):
            done = (met[k, at, 0].astype(F32) + met[k, at ^ 1, 1].astype(F32)).astype(BF16)
            for part in range(SIDE):
                cut[k, part, at * SIDE : (at + 1) * SIDE] = done[:, part * PIECE : (part + 1) * PIECE]
        start(y_spread(k))

    def share(k):
        wait(y_spread(k))
        core_copy(k, 1, spread.at[k, mine], spread.at[k, mine]).start()

    def switch(k):
        core_copy(k, 1, spread.at[k, mine], spread.at[k, mine]).wait()
        for b in range(2 * BLOCKS):
            perm[b] = spread[k, b]
        base = c * BLOCKS
        for i in range(BLOCKS):
            packed[k, i] = perm[moves[base + i]]
        start(y_gather(k))

    def pair(k):
        wait(y_gather(k))
        for at in range(SIDE):
            for i in range(SIDE):
                for part in range(SIDE):
                    pairs[k, at % 2, at // 2, i, part * PIECE : (part + 1) * PIECE] = strips[k, part, at * SIDE + i]
        start(z_gather(k))

    def level_4(k):
        if k == first_chunk(9):
            t_end(4)
        wait(z_gather(k))
        own = lax.div(z, 2)
        now = level_of(4, [s4[k, own, i] for i in range(SIDE)], [s4[k, 1 - own, i] for i in range(SIDE)])
        for i in range(SIDE):
            s5[k, i] = now[i]
        core_copy(k, 2, s5.at[k], p5.at[k]).start()

    def levels_5_7(k):
        if k == first_chunk(10):
            for level in (5, 6, 7):
                t_end(level)
        core_copy(k, 2, s5.at[k], p5.at[k]).wait()
        now = level_of(5, [s5[k, i] for i in range(SIDE)], [p5[k, i] for i in range(SIDE)])
        now = level_of(6, now, [now[i ^ 1] for i in range(SIDE)])
        now = level_of(7, now, [now[i ^ 2] for i in range(SIDE)])
        for i in range(SIDE):
            s8q[k, i] = now[i]
        start(x_out(k))

    def give(k):
        wait(x_out(k))
        keep, first, second, _ = all_copies(k)
        start(first + second + [keep])

    def give_on(k):
        _, first, _, third = all_copies(k)
        for copy, onward in zip(first, third):
            copy.wait()
            onward.start()

    def finish(k):
        keep, _, second, third = all_copies(k)
        wait(second + third + [keep])

    stages = [
        project, relay, total, level_0, levels_1_3, add, share, switch,
        pair, level_4, levels_5_7, give, give_on, finish, t_begin, t_forward,
    ]

    pl.semaphore_wait(barrier, 3 * (SIDE - 1) + 1)
    t_begin(1)
    flip_bases()
    t_swap_begin()
    t_ready(0)
    for stage, at in ORDER:
        stages[stage](at)


def gathered(right_sides, leaf_bases, transfer, ranks, moves):
    dma, vmem = pltpu.SemaphoreType.DMA, pltpu.VMEM
    wide = (CHUNKS, RANK, WIDE)
    half = (CHUNKS, 2, HALF, WIDE)
    parts = (CHUNKS, SIDE, RANK, PART)
    scratch = [
        vmem((CHUNKS, SIDE, RANK, WIDE), F32),
        vmem((SIDE, RANK, RANK), BF16),
        vmem((SIDE, RANK, RANK), BF16),
        vmem((CHUNKS, SIDE, RANK, WIDE), BF16),
        vmem(half, BF16), vmem(half, BF16), vmem(half, BF16), vmem(half, BF16),
        vmem(wide, BF16), vmem(wide, BF16),
        vmem(parts, BF16), vmem(parts, BF16),
        vmem((CHUNKS, SIDE, 2, SIDE, QUARTER, PART), BF16),
        vmem((CHUNKS, SIDE, 2, SIDE, QUARTER, PART), BF16),
        vmem((CHUNKS, SIDE, PLANE, PIECE, PART), BF16),
        vmem((CHUNKS, 2 * BLOCKS, PIECE, PART), BF16),
        vmem((2 * BLOCKS, PIECE, PART), BF16),
        vmem((CHUNKS, BLOCKS, PIECE, PART), BF16),
        vmem((CHUNKS, SIDE, PLANE, PIECE, PART), BF16),
        vmem((CHUNKS, 2, 2, SIDE, QUARTER, PART), BF16),
        vmem((CHUNKS, 2, SIDE, RANK, PART), BF16),
        vmem(parts, BF16), vmem(parts, BF16),
        vmem(parts, BF16), vmem(parts, BF16),
        vmem((LEVELS, SIDE, 2, RANK, RANK), BF16),
        vmem((2, RANK, RANK), BF16),
        dma((CHUNKS,)), dma(()), dma((LEVELS,)), dma((LEVELS, 4)), dma((LEVELS, 4)),
        dma((CHUNKS, 6)), dma((CHUNKS, 6)), dma((CHUNKS, 3)), dma((CHUNKS, 3)),
        dma((CHUNKS, 6, SIDE)), dma((CHUNKS, 6, SIDE)), dma(()), dma(()),
        dma((CHUNKS, 6)), dma((CHUNKS, 7)),
    ]
    anywhere = pl.BlockSpec(memory_space=pl.ANY)
    scalars = pl.BlockSpec(memory_space=pltpu.SMEM)
    return pl.pallas_call(
        butterfly,
        out_shape=jax.ShapeDtypeStruct((SIDE, CHUNKS * SIDE, RANK, PART), BF16),
        in_specs=[anywhere, anywhere, anywhere, scalars, scalars],
        out_specs=anywhere,
        scratch_shapes=scratch,
        compiler_params=pltpu.CompilerParams(
            collective_id=0, has_side_effects=True, vmem_limit_bytes=58 * 1024 * 1024
        ),
        cost_estimate=pl.CostEstimate(
            flops=6 * 10**9, bytes_accessed=24 * 2**20, transcendentals=0
        ),
        name="butterfly",
    )(right_sides, leaf_bases, transfer, ranks, moves)


def expand_block(expand, skeleton, product):
    wide = jnp.concatenate([skeleton[0, part] for part in range(skeleton.shape[1])], axis=1)
    product[0] = dot(expand[0], wide).astype(BF16)


def expanded(leaf_expand, skeleton):
    split = 2
    parts = skeleton.shape[1] // split
    return pl.pallas_call(
        expand_block,
        grid=(SIDE, split),
        out_shape=jax.ShapeDtypeStruct((SIDE, RANK, CHUNKS * WIDE), BF16),
        in_specs=[
            pl.BlockSpec((1, RANK, RANK), lambda j, h: (j, 0, 0)),
            pl.BlockSpec((1, parts, RANK, PART), lambda j, h: (j, h, 0, 0)),
        ],
        out_specs=pl.BlockSpec((1, RANK, parts * PART), lambda j, h: (j, 0, h)),
        compiler_params=pltpu.CompilerParams(vmem_limit_bytes=58 * 1024 * 1024),
        name="expand",
    )(leaf_expand, skeleton)


def switch_table(owner_map):
    place = np.arange(2 * BLOCKS)
    c, y, z, x = place // BLOCKS, place // PLANE % SIDE, place // SIDE % SIDE, place % SIDE
    block_at = (z * (2 * SIDE) + x * 2 + c) * SIDE + y
    place_of = np.zeros_like(place)
    place_of[block_at] = place
    hit = owner_map[None, :] == jnp.asarray(block_at, jnp.int32)[:, None]
    return jnp.sum(jnp.where(hit, jnp.asarray(place_of, jnp.int32)[None, :], 0), axis=1, dtype=jnp.int32)


def local(right_sides, leaf_bases, leaf_expand, transfer, skeleton_ranks, owner_map):
    skeleton = gathered(right_sides, leaf_bases, transfer, skeleton_ranks, switch_table(owner_map))
    return expanded(leaf_expand, skeleton)


def solution(mesh):
    in_specs = (
        P("leaf", "rhs", None),
        P("leaf", "rhs", None),
        P("leaf", "rhs", None),
        P(None, "leaf", None, None, None),
        P(None, "leaf"),
        P(),
    )
    out_specs = P("leaf", "rhs", None)
    return jax.shard_map(local, mesh=mesh, in_specs=in_specs, out_specs=out_specs, check_vma=False)
```

```python
import functools

import jax
import jax.numpy as jnp
from jax import lax
from jax.experimental import pallas as pl
from jax.experimental.pallas import tpu as pltpu
from jax.sharding import PartitionSpec as P

MESH = pl.DeviceIdType.MESH
BF16 = jnp.bfloat16
F32 = jnp.float32

RANK = 256
HALF = RANK // 2
SIDE = 4
CHUNKS = 4
PART = 128
WIDE = SIDE * PART
QUARTER = RANK // SIDE
PIECE = QUARTER // SIDE
PLANE = SIDE * SIDE
BLOCKS = SIDE**3
LEVELS = 8
HALFWAY = 3
LAST = LEVELS - 1

ORDER = [
    (0, 0), (17, 3), (0, 1), (16, 0), (14, 2), (1, 0), (14, 3), (15, 1), (0, 2), (2, 0),
    (1, 1), (15, 2), (3, 0), (1, 2), (15, 3), (0, 3), (16, 7), (18, 0), (2, 1), (3, 1),
    (2, 2), (1, 3), (4, 0), (3, 2), (4, 1), (14, 4), (2, 3), (3, 3), (5, 0), (4, 2),
    (14, 6), (14, 5), (5, 1), (6, 0), (4, 3), (7, 0), (5, 2), (15, 4), (6, 1), (15, 6),
    (7, 1), (8, 0), (6, 2), (15, 5), (5, 3), (8, 1), (7, 2), (9, 0), (6, 3), (10, 0),
    (7, 3), (9, 1), (8, 2), (10, 1), (8, 3), (11, 0), (9, 2), (11, 1), (10, 2), (12, 0),
    (9, 3), (10, 3), (12, 1), (11, 2), (11, 3), (12, 2), (12, 3), (13, 0), (13, 2), (13, 1),
    (13, 3),
]


def first_chunk(stage):
    return next(at for event, at in ORDER if event == stage)


def dot(a, b):
    return jnp.dot(a, b, preferred_element_type=F32)


def butterfly(
    sides, bases, transfer, ranks, owners, out,
    xin, raw, bt, pbuf, rel, direct, fin, acc,
    s0, p0, s1p, s1q, terms, met, cut, spread, perm, packed, strips, pairs, s4, s5, p5, s7q, s7p, s8p, tq, swap, places, moves,
    in_sem, base_sem, t_sem, table_sem, tx_send, tx_recv,
    rs_send, rs_recv, core_send, core_recv, all_send, all_recv, swap_send, swap_recv, ag_send, ag_recv,
):
    leaf = lax.axis_index("leaf")
    y = lax.axis_index("rhs")
    c = lax.rem(leaf, 2)
    x = lax.rem(lax.div(leaf, 2), SIDE)
    z = lax.div(leaf, 2 * SIDE)

    def device(z_at, x_at, c_at, y_at):
        return {"leaf": z_at * (2 * SIDE) + x_at * 2 + c_at, "rhs": y_at}

    def turn(at, by):
        return lax.rem(at + by, SIDE)

    def remote(src, dst, send, recv, to):
        return pltpu.make_async_remote_copy(
            src_ref=src, dst_ref=dst, send_sem=send, recv_sem=recv, device_id=to, device_id_type=MESH
        )

    up, down = device(z, x, c, turn(y, 1)), device(z, x, c, turn(y, 3))
    twin = device(z, x, 1 - c, y)
    z_near = device(z + 1 - 2 * lax.rem(z, 2), x, c, y)
    x_right, x_left = device(z, turn(x, 1), c, y), device(z, turn(x, 3), c, y)

    barrier = pltpu.get_barrier_semaphore()
    for by in range(1, SIDE):
        for peer in (device(turn(z, by), x, c, y), device(z, turn(x, by), c, y), device(z, x, c, turn(y, by))):
            pl.semaphore_signal(barrier, inc=1, device_id=peer, device_id_type=MESH)
    pl.semaphore_signal(barrier, inc=1, device_id=twin, device_id_type=MESH)

    def load_sides(k):
        return pltpu.make_async_copy(
            sides.at[:, :, pl.ds(pl.multiple_of(k * WIDE, WIDE), WIDE)], xin.at[k], in_sem.at[k]
        )

    def load_transfer(level):
        land = swap if level == HALFWAY else tq.at[level, x]
        return pltpu.make_async_copy(transfer.at[level, y], land, t_sem.at[level])

    load_bases = pltpu.make_async_copy(bases, raw, base_sem)
    load_transfer(1).start()
    load_bases.start()
    load_sides(0).start()

    def load_rest():
        load_transfer(HALFWAY).start()
        load_transfer(2).start()
        load_sides(1).start()
        load_transfer(0).start()
        for k in range(2, CHUNKS):
            load_sides(k).start()
        for level in range(HALFWAY + 1, LEVELS):
            load_transfer(level).start()

    rows = lax.broadcasted_iota(jnp.int32, (RANK, RANK), 0)
    slot_ids = lax.broadcasted_iota(jnp.int32, ranks.shape, 0)
    own_ranks = jnp.sum(jnp.where(slot_ids == y, ranks[...], 0), axis=0, keepdims=True)

    def flip_bases():
        load_bases.wait()
        for j in range(SIDE):
            flipped = raw[j].astype(F32).T
            bt[j] = jnp.where(rows < ranks[j : j + 1, 0:1], flipped, 0.0).astype(BF16)

    table = pltpu.make_async_copy(places, moves, table_sem)

    def switch_table(_):
        at = lax.broadcasted_iota(jnp.int32, (2 * BLOCKS, 2 * BLOCKS), 1)
        block_at = (at // SIDE % SIDE) * (2 * PLANE) + (at % SIDE) * (2 * SIDE) + (at // BLOCKS) * SIDE + at // PLANE % SIDE
        block = lax.broadcasted_iota(jnp.int32, (2 * BLOCKS, 2 * BLOCKS), 0)
        place = (
            (block // SIDE % 2) * BLOCKS + (block % SIDE) * PLANE + (block // (2 * PLANE)) * SIDE
            + block // (2 * SIDE) % SIDE
        )
        goes_to = jnp.broadcast_to(owners[...].astype(F32), at.shape).T.astype(jnp.int32)
        places[...] = jnp.sum(jnp.where(goes_to == block_at, place, 0), axis=0, keepdims=True)
        table.start()

    def t_right(level):
        return remote(tq.at[level, x], tq.at[level, x], tx_send.at[level, 0], tx_recv.at[level, 0], x_right)

    def t_left(level):
        return remote(tq.at[level, x], tq.at[level, x], tx_send.at[level, 1], tx_recv.at[level, 1], x_left)

    def t_on_right(level):
        part = tq.at[level, turn(x, 3), 0]
        return remote(part, part, tx_send.at[level, 2], tx_recv.at[level, 2], x_right)

    def t_on_left(level):
        part = tq.at[level, turn(x, 1), 1]
        return remote(part, part, tx_send.at[level, 3], tx_recv.at[level, 3], x_left)

    def masked(level, matrix):
        return jnp.where(rows < own_ranks[:, level + 1 : level + 2], matrix.astype(F32), 0.0).astype(BF16)

    def t_ready(level):
        load_transfer(level).wait()
        for side in range(2):
            tq[level, x, side] = masked(level, tq[level, x, side])

    t_swap = remote(swap.at[1], tq.at[HALFWAY, x, 1], swap_send, swap_recv, z_near)

    def t_swap_begin(_):
        load_transfer(HALFWAY).wait()
        tq[HALFWAY, x, 0] = masked(HALFWAY, swap[0])
        swap[1] = masked(HALFWAY, swap[1])
        t_swap.start()

    def t_begin(level):
        if level == HALFWAY:
            t_swap.wait()
        else:
            t_ready(level)
        t_right(level).start()
        t_left(level).start()

    def t_forward(level):
        t_right(level).wait()
        t_left(level).wait()
        t_on_right(level).start()
        t_on_left(level).start()

    def t_end(level):
        t_on_right(level).wait()
        t_on_left(level).wait()

    low, high = pl.ds(0, HALF), pl.ds(HALF, HALF)

    def sum_copies(k):
        across, above, below = turn(y, 2), turn(y, 1), turn(y, 3)
        first = [
            remote(pbuf.at[k, across, low], rel.at[k, 0], rs_send.at[k, 0], rs_recv.at[k, 0], down),
            remote(pbuf.at[k, across, high], rel.at[k, 1], rs_send.at[k, 1], rs_recv.at[k, 1], up),
        ]
        near_up = remote(pbuf.at[k, above, low], direct.at[k, 0], rs_send.at[k, 2], rs_recv.at[k, 2], up)
        near_down = remote(pbuf.at[k, below, high], direct.at[k, 1], rs_send.at[k, 3], rs_recv.at[k, 3], down)
        second = [
            remote(acc.at[k, 0], fin.at[k, 0], rs_send.at[k, 4], rs_recv.at[k, 4], down),
            remote(acc.at[k, 1], fin.at[k, 1], rs_send.at[k, 5], rs_recv.at[k, 5], up),
        ]
        return first, near_up, near_down, second

    def core_copy(k, n, src, dst):
        return remote(src, dst, core_send.at[k, n], core_recv.at[k, n], twin)

    def every(k, n, src_of, dst, me, device_of):
        copies = [pltpu.make_async_copy(src_of(me), dst, all_recv.at[k, n, 0])]
        for by in range(1, SIDE):
            to = turn(me, by)
            copies.append(remote(src_of(to), dst, all_send.at[k, n, by], all_recv.at[k, n, by], device_of(to)))
        return copies

    def along_x(k, n, src_of, dst):
        return every(k, n, src_of, dst, x, lambda to: device(z, to, c, y))

    def along_y(k, n, src_of, dst):
        return every(k, n, src_of, dst, y, lambda to: device(z, x, c, to))

    def along_z(k, n, src_of, dst):
        return every(k, n, src_of, dst, z, lambda to: device(to, x, c, y))

    def x_in(k):
        return along_x(k, 0, lambda to: s1p.at[k, to], s1q.at[k, x])

    def z_spread(k):
        return along_z(k, 1, lambda to: terms.at[k, to], met.at[k, z])

    def y_spread(k):
        land = spread.at[k, pl.ds(c * BLOCKS + y * PLANE, PLANE)]
        return along_y(k, 2, lambda to: cut.at[k, to], land)

    def y_gather(k):
        return along_y(k, 3, lambda to: packed.at[k, pl.ds(to * PLANE, PLANE)], strips.at[k, y])

    def z_gather(k):
        land = s4.at[k, :, :, pl.ds(pl.multiple_of(z * QUARTER, QUARTER), QUARTER)]
        return along_z(k, 4, lambda to: pairs.at[k, lax.rem(to, 2)], land)

    def x_out(k):
        return along_x(k, 5, lambda to: s7q.at[k, lax.rem(to, 2)], s7p.at[k, x])

    mine = pl.ds(c * BLOCKS, BLOCKS)

    def start(copies):
        for copy in copies:
            copy.start()

    def wait(copies):
        for copy in copies:
            copy.wait()

    def columns_of(k):
        return pl.ds(k * SIDE, SIDE)

    def all_copies(k):
        columns = columns_of(k)
        keep = pltpu.make_async_copy(s8p.at[k], out.at[y, columns], ag_recv.at[k, 6])

        def give(n, half, to):
            return remote(
                s8p.at[k, :, half], out.at[y, columns, half], ag_send.at[k, n], ag_recv.at[k, n], to
            )

        def onward(n, at, half, to):
            part = out.at[at, columns, half]
            return remote(part, part, ag_send.at[k, n], ag_recv.at[k, n], to)

        first = [give(0, low, up), give(1, high, down)]
        second = [give(2, high, up), give(3, low, down)]
        third = [onward(4, turn(y, 3), low, up), onward(5, turn(y, 1), high, down)]
        return keep, first, second, third

    def level_of(level, near, far):
        return [
            (dot(tq[level, i, 0], near[i]) + dot(tq[level, i, 1], far[i])).astype(BF16) for i in range(SIDE)
        ]

    def project(k):
        load_sides(k).wait()
        first, near_up, near_down, _ = sum_copies(k)
        for by, copies in ((2, first), (1, [near_up]), (3, [near_down]), (0, [])):
            j = turn(y, by)
            pbuf[k, j] = dot(bt[j], xin[k, j].astype(BF16)).astype(BF16)
            for copy in copies:
                copy.start()

    def relay(k):
        first, _, _, second = sum_copies(k)
        first[0].wait()
        acc[k, 0] = (rel[k, 0].astype(F32) + pbuf[k, turn(y, 3), :HALF].astype(F32)).astype(BF16)
        second[0].start()
        first[1].wait()
        acc[k, 1] = (rel[k, 1].astype(F32) + pbuf[k, turn(y, 1), HALF:].astype(F32)).astype(BF16)
        second[1].start()

    def total(k):
        _, near_up, near_down, second = sum_copies(k)
        for copy in (near_up, near_down, *second):
            copy.wait()
        for half in range(2):
            at = pl.ds(half * HALF, HALF)
            s0[k, at] = (
                pbuf[k, y, at].astype(F32) + direct[k, half].astype(F32) + fin[k, half].astype(F32)
            ).astype(BF16)
        core_copy(k, 0, s0.at[k], p0.at[k]).start()

    def level_0(k):
        core_copy(k, 0, s0.at[k], p0.at[k]).wait()
        done = (dot(tq[0, x, 0], s0[k]) + dot(tq[0, x, 1], p0[k])).astype(BF16)
        for part in range(SIDE):
            s1p[k, part] = done[:, part * PART : (part + 1) * PART]
        start(x_in(k))

    def levels_1_3(k):
        if k == first_chunk(4):
            for level in (1, 2, 3):
                t_end(level)
        wait(x_in(k))
        now = [s1q[k, i] for i in range(SIDE)]
        now = level_of(1, now, [now[i ^ 1] for i in range(SIDE)])
        now = level_of(2, now, [now[i ^ 2] for i in range(SIDE)])
        for i in range(SIDE):
            for side in range(2):
                term = dot(tq[HALFWAY, i, side], now[i]).astype(BF16)
                for part in range(SIDE):
                    terms[k, part, side, i] = term[part * QUARTER : (part + 1) * QUARTER]
        start(z_spread(k))

    def add(k):
        wait(z_spread(k))
        for at in range(SIDE):
            done = (met[k, at, 0].astype(F32) + met[k, at ^ 1, 1].astype(F32)).astype(BF16)
            for part in range(SIDE):
                cut[k, part, at * SIDE : (at + 1) * SIDE] = done[:, part * PIECE : (part + 1) * PIECE]
        start(y_spread(k))

    def share(k):
        wait(y_spread(k))
        core_copy(k, 1, spread.at[k, mine], spread.at[k, mine]).start()

    def switch(k):
        if k == first_chunk(7):
            table.wait()
        core_copy(k, 1, spread.at[k, mine], spread.at[k, mine]).wait()
        for b in range(2 * BLOCKS):
            perm[b] = spread[k, b]
        base = c * BLOCKS
        for i in range(BLOCKS):
            packed[k, i] = perm[moves[0, base + i]]
        start(y_gather(k))

    def pair(k):
        wait(y_gather(k))
        for at in range(SIDE):
            for i in range(SIDE):
                for part in range(SIDE):
                    pairs[k, at % 2, at // 2, i, part * PIECE : (part + 1) * PIECE] = strips[k, part, at * SIDE + i]
        start(z_gather(k))

    def level_4(k):
        if k == first_chunk(9):
            t_end(4)
        wait(z_gather(k))
        own = lax.div(z, 2)
        now = level_of(4, [s4[k, own, i] for i in range(SIDE)], [s4[k, 1 - own, i] for i in range(SIDE)])
        for i in range(SIDE):
            s5[k, i] = now[i]
        core_copy(k, 2, s5.at[k], p5.at[k]).start()

    def levels_5_6(k):
        if k == first_chunk(10):
            for level in (5, 6):
                t_end(level)
        core_copy(k, 2, s5.at[k], p5.at[k]).wait()
        now = level_of(5, [s5[k, i] for i in range(SIDE)], [p5[k, i] for i in range(SIDE)])
        now = level_of(6, now, [now[i ^ 1] for i in range(SIDE)])
        for i in range(SIDE):
            s7q[k, i % 2, i // 2] = now[i]
        start(x_out(k))

    def give(k):
        wait(x_out(k))
        own = lax.div(x, 2)
        for part in range(SIDE):
            s8p[k, part] = (
                dot(tq[LAST, x, 0], s7p[k, part, own]) + dot(tq[LAST, x, 1], s7p[k, part, 1 - own])
            ).astype(BF16)
        keep, first, second, _ = all_copies(k)
        start(first + second + [keep])

    def give_on(k):
        _, first, _, third = all_copies(k)
        for copy, onward in zip(first, third):
            copy.wait()
            onward.start()

    def finish(k):
        keep, _, second, third = all_copies(k)
        wait(second + third + [keep])

    stages = [
        project, relay, total, level_0, levels_1_3, add, share, switch,
        pair, level_4, levels_5_6, give, give_on, finish, t_begin, t_forward, t_ready, t_swap_begin, switch_table,
    ]

    flip_bases()
    pl.semaphore_wait(barrier, 3 * (SIDE - 1) + 1)
    t_begin(1)
    load_rest()
    for stage, at in ORDER:
        stages[stage](at)


def gathered(right_sides, leaf_bases, transfer, ranks, owners):
    dma, vmem = pltpu.SemaphoreType.DMA, pltpu.VMEM
    wide = (CHUNKS, RANK, WIDE)
    half = (CHUNKS, 2, HALF, WIDE)
    parts = (CHUNKS, SIDE, RANK, PART)
    scratch = [
        vmem((CHUNKS, SIDE, RANK, WIDE), F32),
        vmem((SIDE, RANK, RANK), BF16),
        vmem((SIDE, RANK, RANK), BF16),
        vmem((CHUNKS, SIDE, RANK, WIDE), BF16),
        vmem(half, BF16), vmem(half, BF16), vmem(half, BF16), vmem(half, BF16),
        vmem(wide, BF16), vmem(wide, BF16),
        vmem(parts, BF16), vmem(parts, BF16),
        vmem((CHUNKS, SIDE, 2, SIDE, QUARTER, PART), BF16),
        vmem((CHUNKS, SIDE, 2, SIDE, QUARTER, PART), BF16),
        vmem((CHUNKS, SIDE, PLANE, PIECE, PART), BF16),
        vmem((CHUNKS, 2 * BLOCKS, PIECE, PART), BF16),
        vmem((2 * BLOCKS, PIECE, PART), BF16),
        vmem((CHUNKS, BLOCKS, PIECE, PART), BF16),
        vmem((CHUNKS, SIDE, PLANE, PIECE, PART), BF16),
        vmem((CHUNKS, 2, 2, SIDE, QUARTER, PART), BF16),
        vmem((CHUNKS, 2, SIDE, RANK, PART), BF16),
        vmem(parts, BF16), vmem(parts, BF16),
        vmem((CHUNKS, 2, 2, RANK, PART), BF16), vmem((CHUNKS, SIDE, 2, RANK, PART), BF16),
        vmem(parts, BF16),
        vmem((LEVELS, SIDE, 2, RANK, RANK), BF16),
        vmem((2, RANK, RANK), BF16),
        vmem((1, 2 * BLOCKS), jnp.int32), pltpu.SMEM((1, 2 * BLOCKS), jnp.int32),
        dma((CHUNKS,)), dma(()), dma((LEVELS,)), dma(()), dma((LEVELS, 4)), dma((LEVELS, 4)),
        dma((CHUNKS, 6)), dma((CHUNKS, 6)), dma((CHUNKS, 3)), dma((CHUNKS, 3)),
        dma((CHUNKS, 6, SIDE)), dma((CHUNKS, 6, SIDE)), dma(()), dma(()),
        dma((CHUNKS, 6)), dma((CHUNKS, 7)),
    ]
    anywhere = pl.BlockSpec(memory_space=pl.ANY)
    in_vmem = pl.BlockSpec(memory_space=pltpu.VMEM)
    return pl.pallas_call(
        butterfly,
        out_shape=jax.ShapeDtypeStruct((SIDE, CHUNKS * SIDE, RANK, PART), BF16),
        in_specs=[anywhere, anywhere, anywhere, in_vmem, in_vmem],
        out_specs=anywhere,
        scratch_shapes=scratch,
        compiler_params=pltpu.CompilerParams(
            collective_id=0, has_side_effects=True, vmem_limit_bytes=58 * 1024 * 1024
        ),
        cost_estimate=pl.CostEstimate(
            flops=6 * 10**9, bytes_accessed=24 * 2**20, transcendentals=0
        ),
        name="butterfly",
    )(right_sides, leaf_bases, transfer, ranks, owners)


def expand_blocks(expand, skeleton, product, weights, tiles, done, in_sem, out_sem):
    loads = [
        (
            pltpu.make_async_copy(expand.at[j], weights.at[j], in_sem.at[j, 0]),
            pltpu.make_async_copy(skeleton.at[j], tiles.at[j], in_sem.at[j, 1]),
        )
        for j in range(SIDE)
    ]
    stores = [pltpu.make_async_copy(done.at[j], product.at[j], out_sem.at[j]) for j in range(SIDE)]
    for pair in loads:
        for copy in pair:
            copy.start()
    for j in range(SIDE):
        for copy in loads[j]:
            copy.wait()
        wide = jnp.concatenate([tiles[j, part] for part in range(CHUNKS * SIDE)], axis=1)
        done[j] = dot(weights[j], wide).astype(BF16)
        stores[j].start()
    for copy in stores:
        copy.wait()


def expanded(leaf_expand, skeleton):
    dma, vmem = pltpu.SemaphoreType.DMA, pltpu.VMEM
    anywhere = pl.BlockSpec(memory_space=pl.ANY)
    product = (SIDE, RANK, CHUNKS * WIDE)
    return pl.pallas_call(
        expand_blocks,
        out_shape=jax.ShapeDtypeStruct(product, BF16),
        in_specs=[anywhere, anywhere],
        out_specs=anywhere,
        scratch_shapes=[
            vmem(leaf_expand.shape, BF16), vmem(skeleton.shape, BF16), vmem(product, BF16),
            dma((SIDE, 2)), dma((SIDE,)),
        ],
        compiler_params=pltpu.CompilerParams(vmem_limit_bytes=58 * 1024 * 1024),
        name="expand",
    )(leaf_expand, skeleton)


def local(right_sides, leaf_bases, leaf_expand, transfer, skeleton_ranks, owner_map):
    skeleton = gathered(right_sides, leaf_bases, transfer, skeleton_ranks.T, owner_map[None, :])
    return expanded(leaf_expand, skeleton)


def solution(mesh):
    in_specs = (
        P("leaf", "rhs", None),
        P("leaf", "rhs", None),
        P("leaf", "rhs", None),
        P(None, "leaf", None, None, None),
        P(None, "leaf"),
        P(),
    )
    out_specs = P("leaf", "rhs", None)
    return jax.shard_map(local, mesh=mesh, in_specs=in_specs, out_specs=out_specs, check_vma=False)
```

```python
import functools

import jax
import jax.numpy as jnp
from jax import lax
from jax.experimental import pallas as pl
from jax.experimental.pallas import tpu as pltpu
from jax.sharding import PartitionSpec as P

MESH = pl.DeviceIdType.MESH
BF16 = jnp.bfloat16
F32 = jnp.float32

RANK = 256
HALF = RANK // 2
SIDE = 4
CHUNKS = 4
PART = 128
WIDE = SIDE * PART
QUARTER = RANK // SIDE
PIECE = QUARTER // SIDE
PLANE = SIDE * SIDE
BLOCKS = SIDE**3
LEVELS = 8
SLOTS = (2, 1, 3, 0)
HALFWAY = 3
LAST = LEVELS - 1

ORDER = [
    (0, 0), (17, 3), (0, 1), (16, 0), (14, 2), (1, 0), (14, 3), (1, 1), (0, 2), (15, 1),
    (2, 0), (15, 2), (0, 3), (16, 7), (18, 0), (3, 0), (1, 2), (15, 3), (2, 1), (3, 1),
    (14, 4), (1, 3), (4, 0), (2, 2), (4, 1), (3, 2), (2, 3), (3, 3), (5, 0), (14, 6),
    (4, 2), (5, 1), (14, 5), (6, 0), (15, 4), (4, 3), (7, 0), (5, 2), (6, 1), (7, 1),
    (15, 6), (8, 0), (5, 3), (6, 2), (15, 5), (8, 1), (7, 2), (6, 3), (9, 0), (10, 0),
    (8, 2), (7, 3), (9, 1), (10, 1), (8, 3), (11, 0), (9, 2), (10, 2), (11, 1), (12, 0),
    (9, 3), (10, 3), (11, 2), (12, 1), (11, 3), (12, 2), (12, 3), (13, 0), (13, 1), (13, 2),
    (13, 3),
]


def first_chunk(stage):
    return next(at for event, at in ORDER if event == stage)


def dot(a, b):
    return jnp.dot(a, b, preferred_element_type=F32)


def butterfly(
    sides, bases, transfer, ranks, owners, out,
    xin, raw, bt, pbuf, rel, direct, fin, acc,
    s0, p0, s1p, s1q, terms, met, cut, spread, perm, packed, strips, pairs, s4, s5, p5, s7q, s7p, s8p, tq, swap, places, moves,
    in_sem, base_sem, t_sem, table_sem, tx_send, tx_recv,
    rs_send, rs_recv, core_send, core_recv, all_send, all_recv, swap_send, swap_recv, ag_send, ag_recv,
):
    leaf = lax.axis_index("leaf")
    y = lax.axis_index("rhs")
    c = lax.rem(leaf, 2)
    x = lax.rem(lax.div(leaf, 2), SIDE)
    z = lax.div(leaf, 2 * SIDE)

    def device(z_at, x_at, c_at, y_at):
        return {"leaf": z_at * (2 * SIDE) + x_at * 2 + c_at, "rhs": y_at}

    def turn(at, by):
        return lax.rem(at + by, SIDE)

    def remote(src, dst, send, recv, to):
        return pltpu.make_async_remote_copy(
            src_ref=src, dst_ref=dst, send_sem=send, recv_sem=recv, device_id=to, device_id_type=MESH
        )

    up, down = device(z, x, c, turn(y, 1)), device(z, x, c, turn(y, 3))
    twin = device(z, x, 1 - c, y)
    z_near = device(z + 1 - 2 * lax.rem(z, 2), x, c, y)
    x_right, x_left = device(z, turn(x, 1), c, y), device(z, turn(x, 3), c, y)

    barrier = pltpu.get_barrier_semaphore()
    for by in range(1, SIDE):
        for peer in (device(turn(z, by), x, c, y), device(z, turn(x, by), c, y), device(z, x, c, turn(y, by))):
            pl.semaphore_signal(barrier, inc=1, device_id=peer, device_id_type=MESH)
    pl.semaphore_signal(barrier, inc=1, device_id=twin, device_id_type=MESH)

    def load_sides(k, by):
        j = turn(y, by)
        return pltpu.make_async_copy(sides.at[j, :, pl.ds(k * WIDE, WIDE)], xin.at[k, j], in_sem.at[k, by])

    def load_transfer(level):
        land = swap if level == HALFWAY else tq.at[level, x]
        return pltpu.make_async_copy(transfer.at[level, y], land, t_sem.at[level])

    load_bases = pltpu.make_async_copy(bases, raw, base_sem)
    load_transfer(1).start()
    load_bases.start()
    for by in SLOTS:
        load_sides(0, by).start()

    def load_rest():
        load_transfer(HALFWAY).start()
        load_transfer(2).start()
        for by in SLOTS:
            load_sides(1, by).start()
        load_transfer(0).start()
        for k in range(2, CHUNKS):
            for by in SLOTS:
                load_sides(k, by).start()
        for level in range(HALFWAY + 1, LEVELS):
            load_transfer(level).start()

    rows = lax.broadcasted_iota(jnp.int32, (RANK, RANK), 0)
    slot_ids = lax.broadcasted_iota(jnp.int32, ranks.shape, 0)
    own_ranks = jnp.sum(jnp.where(slot_ids == y, ranks[...], 0), axis=0, keepdims=True)

    def flip_bases(j):
        of_slot = jnp.sum(jnp.where(slot_ids == j, ranks[...], 0), axis=0, keepdims=True)
        bt[j] = jnp.where(rows < of_slot[:, 0:1], raw[j].astype(F32).T, 0.0).astype(BF16)

    table = pltpu.make_async_copy(places, moves, table_sem)

    def switch_table(_):
        at = lax.broadcasted_iota(jnp.int32, (2 * BLOCKS, 2 * BLOCKS), 1)
        block_at = (at // SIDE % SIDE) * (2 * PLANE) + (at % SIDE) * (2 * SIDE) + (at // BLOCKS) * SIDE + at // PLANE % SIDE
        block = lax.broadcasted_iota(jnp.int32, (2 * BLOCKS, 2 * BLOCKS), 0)
        place = (
            (block // SIDE % 2) * BLOCKS + (block % SIDE) * PLANE + (block // (2 * PLANE)) * SIDE
            + block // (2 * SIDE) % SIDE
        )
        goes_to = jnp.broadcast_to(owners[...].astype(F32), at.shape).T.astype(jnp.int32)
        places[...] = jnp.sum(jnp.where(goes_to == block_at, place, 0), axis=0, keepdims=True)
        table.start()

    def t_right(level):
        return remote(tq.at[level, x], tq.at[level, x], tx_send.at[level, 0], tx_recv.at[level, 0], x_right)

    def t_left(level):
        return remote(tq.at[level, x], tq.at[level, x], tx_send.at[level, 1], tx_recv.at[level, 1], x_left)

    def t_on_right(level):
        part = tq.at[level, turn(x, 3), 0]
        return remote(part, part, tx_send.at[level, 2], tx_recv.at[level, 2], x_right)

    def t_on_left(level):
        part = tq.at[level, turn(x, 1), 1]
        return remote(part, part, tx_send.at[level, 3], tx_recv.at[level, 3], x_left)

    def masked(level, matrix):
        return jnp.where(rows < own_ranks[:, level + 1 : level + 2], matrix.astype(F32), 0.0).astype(BF16)

    def t_ready(level):
        load_transfer(level).wait()
        for side in range(2):
            tq[level, x, side] = masked(level, tq[level, x, side])

    t_swap = remote(swap.at[1], tq.at[HALFWAY, x, 1], swap_send, swap_recv, z_near)

    def t_swap_begin(_):
        load_transfer(HALFWAY).wait()
        tq[HALFWAY, x, 0] = masked(HALFWAY, swap[0])
        swap[1] = masked(HALFWAY, swap[1])
        t_swap.start()

    def t_begin(level):
        if level == HALFWAY:
            t_swap.wait()
        else:
            t_ready(level)
        t_right(level).start()
        t_left(level).start()

    def t_forward(level):
        t_right(level).wait()
        t_left(level).wait()
        t_on_right(level).start()
        t_on_left(level).start()

    def t_end(level):
        t_on_right(level).wait()
        t_on_left(level).wait()

    low, high = pl.ds(0, HALF), pl.ds(HALF, HALF)

    def sum_copies(k):
        across, above, below = turn(y, 2), turn(y, 1), turn(y, 3)
        first = [
            remote(pbuf.at[k, across, low], rel.at[k, 0], rs_send.at[k, 0], rs_recv.at[k, 0], down),
            remote(pbuf.at[k, across, high], rel.at[k, 1], rs_send.at[k, 1], rs_recv.at[k, 1], up),
        ]
        near_up = remote(pbuf.at[k, above, low], direct.at[k, 0], rs_send.at[k, 2], rs_recv.at[k, 2], up)
        near_down = remote(pbuf.at[k, below, high], direct.at[k, 1], rs_send.at[k, 3], rs_recv.at[k, 3], down)
        second = [
            remote(acc.at[k, 0], fin.at[k, 0], rs_send.at[k, 4], rs_recv.at[k, 4], down),
            remote(acc.at[k, 1], fin.at[k, 1], rs_send.at[k, 5], rs_recv.at[k, 5], up),
        ]
        return first, near_up, near_down, second

    def core_copy(k, n, src, dst):
        return remote(src, dst, core_send.at[k, n], core_recv.at[k, n], twin)

    def every(k, n, src_of, dst, me, device_of):
        copies = []
        for by in SLOTS[:-1]:
            to = turn(me, by)
            copies.append(remote(src_of(to), dst, all_send.at[k, n, by], all_recv.at[k, n, by], device_of(to)))
        return copies + [pltpu.make_async_copy(src_of(me), dst, all_recv.at[k, n, 0])]

    def along_x(k, n, src_of, dst):
        return every(k, n, src_of, dst, x, lambda to: device(z, to, c, y))

    def along_y(k, n, src_of, dst):
        return every(k, n, src_of, dst, y, lambda to: device(z, x, c, to))

    def along_z(k, n, src_of, dst):
        return every(k, n, src_of, dst, z, lambda to: device(to, x, c, y))

    def x_in(k):
        return along_x(k, 0, lambda to: s1p.at[k, to], s1q.at[k, x])

    def z_spread(k):
        return along_z(k, 1, lambda to: terms.at[k, to], met.at[k, z])

    def y_spread(k):
        land = spread.at[k, pl.ds(c * BLOCKS + y * PLANE, PLANE)]
        return along_y(k, 2, lambda to: cut.at[k, to], land)

    def y_gather(k):
        return along_y(k, 3, lambda to: packed.at[k, pl.ds(to * PLANE, PLANE)], strips.at[k, y])

    def z_gather(k):
        land = s4.at[k, :, :, pl.ds(pl.multiple_of(z * QUARTER, QUARTER), QUARTER)]
        return along_z(k, 4, lambda to: pairs.at[k, lax.rem(to, 2)], land)

    def x_out(k):
        return along_x(k, 5, lambda to: s7q.at[k, lax.rem(to, 2)], s7p.at[k, x])

    mine = pl.ds(c * BLOCKS, BLOCKS)

    def start(copies):
        for copy in copies:
            copy.start()

    def wait(copies):
        for copy in copies:
            copy.wait()

    def columns_of(k):
        return pl.ds(k * SIDE, SIDE)

    def all_copies(k):
        columns = columns_of(k)
        keep = pltpu.make_async_copy(s8p.at[k], out.at[y, columns], ag_recv.at[k, 6])

        def give(n, half, to):
            return remote(
                s8p.at[k, :, half], out.at[y, columns, half], ag_send.at[k, n], ag_recv.at[k, n], to
            )

        def onward(n, at, half, to):
            part = out.at[at, columns, half]
            return remote(part, part, ag_send.at[k, n], ag_recv.at[k, n], to)

        first = [give(0, low, up), give(1, high, down)]
        second = [give(2, high, up), give(3, low, down)]
        third = [onward(4, turn(y, 3), low, up), onward(5, turn(y, 1), high, down)]
        return keep, first, second, third

    def level_of(level, near, far):
        return [
            (dot(tq[level, i, 0], near[i]) + dot(tq[level, i, 1], far[i])).astype(BF16) for i in range(SIDE)
        ]

    def project(k):
        if k == first_chunk(0):
            load_bases.wait()
        first, near_up, near_down, _ = sum_copies(k)
        for by, copies in zip(SLOTS, (first, [near_up], [near_down], [])):
            j = turn(y, by)
            if k == first_chunk(0):
                flip_bases(j)
            load_sides(k, by).wait()
            pbuf[k, j] = dot(bt[j], xin[k, j].astype(BF16)).astype(BF16)
            for copy in copies:
                copy.start()

    def relay(k):
        first, _, _, second = sum_copies(k)
        first[0].wait()
        acc[k, 0] = (rel[k, 0].astype(F32) + pbuf[k, turn(y, 3), :HALF].astype(F32)).astype(BF16)
        second[0].start()
        first[1].wait()
        acc[k, 1] = (rel[k, 1].astype(F32) + pbuf[k, turn(y, 1), HALF:].astype(F32)).astype(BF16)
        second[1].start()

    def total(k):
        _, near_up, near_down, second = sum_copies(k)
        for copy in (near_up, near_down, *second):
            copy.wait()
        for half in range(2):
            at = pl.ds(half * HALF, HALF)
            s0[k, at] = (
                pbuf[k, y, at].astype(F32) + direct[k, half].astype(F32) + fin[k, half].astype(F32)
            ).astype(BF16)
        core_copy(k, 0, s0.at[k], p0.at[k]).start()

    def level_0(k):
        core_copy(k, 0, s0.at[k], p0.at[k]).wait()
        done = (dot(tq[0, x, 0], s0[k]) + dot(tq[0, x, 1], p0[k])).astype(BF16)
        for part in range(SIDE):
            s1p[k, part] = done[:, part * PART : (part + 1) * PART]
        start(x_in(k))

    def levels_1_3(k):
        if k == first_chunk(4):
            for level in (1, 2, 3):
                t_end(level)
        wait(x_in(k))
        now = [s1q[k, i] for i in range(SIDE)]
        now = level_of(1, now, [now[i ^ 1] for i in range(SIDE)])
        now = level_of(2, now, [now[i ^ 2] for i in range(SIDE)])
        for i in range(SIDE):
            for side in range(2):
                term = dot(tq[HALFWAY, i, side], now[i]).astype(BF16)
                for part in range(SIDE):
                    terms[k, part, side, i] = term[part * QUARTER : (part + 1) * QUARTER]
        start(z_spread(k))

    def add(k):
        wait(z_spread(k))
        for at in range(SIDE):
            done = (met[k, at, 0].astype(F32) + met[k, at ^ 1, 1].astype(F32)).astype(BF16)
            for part in range(SIDE):
                cut[k, part, at * SIDE : (at + 1) * SIDE] = done[:, part * PIECE : (part + 1) * PIECE]
        start(y_spread(k))

    def share(k):
        wait(y_spread(k))
        core_copy(k, 1, spread.at[k, mine], spread.at[k, mine]).start()

    def switch(k):
        if k == first_chunk(7):
            table.wait()
        core_copy(k, 1, spread.at[k, mine], spread.at[k, mine]).wait()
        for b in range(2 * BLOCKS):
            perm[b] = spread[k, b]
        base = c * BLOCKS
        for i in range(BLOCKS):
            packed[k, i] = perm[moves[0, base + i]]
        start(y_gather(k))

    def pair(k):
        wait(y_gather(k))
        for at in range(SIDE):
            for i in range(SIDE):
                for part in range(SIDE):
                    pairs[k, at % 2, at // 2, i, part * PIECE : (part + 1) * PIECE] = strips[k, part, at * SIDE + i]
        start(z_gather(k))

    def level_4(k):
        if k == first_chunk(9):
            t_end(4)
        wait(z_gather(k))
        own = lax.div(z, 2)
        now = level_of(4, [s4[k, own, i] for i in range(SIDE)], [s4[k, 1 - own, i] for i in range(SIDE)])
        for i in range(SIDE):
            s5[k, i] = now[i]
        core_copy(k, 2, s5.at[k], p5.at[k]).start()

    def levels_5_6(k):
        if k == first_chunk(10):
            for level in (5, 6):
                t_end(level)
        core_copy(k, 2, s5.at[k], p5.at[k]).wait()
        now = level_of(5, [s5[k, i] for i in range(SIDE)], [p5[k, i] for i in range(SIDE)])
        now = level_of(6, now, [now[i ^ 1] for i in range(SIDE)])
        for i in range(SIDE):
            s7q[k, i % 2, i // 2] = now[i]
        start(x_out(k))

    def give(k):
        wait(x_out(k))
        own = lax.div(x, 2)
        for part in range(SIDE):
            s8p[k, part] = (
                dot(tq[LAST, x, 0], s7p[k, part, own]) + dot(tq[LAST, x, 1], s7p[k, part, 1 - own])
            ).astype(BF16)
        keep, first, second, _ = all_copies(k)
        start(first + second + [keep])

    def give_on(k):
        _, first, _, third = all_copies(k)
        for copy, onward in zip(first, third):
            copy.wait()
            onward.start()

    def finish(k):
        keep, _, second, third = all_copies(k)
        wait(second + third + [keep])

    stages = [
        project, relay, total, level_0, levels_1_3, add, share, switch,
        pair, level_4, levels_5_6, give, give_on, finish, t_begin, t_forward, t_ready, t_swap_begin, switch_table,
    ]

    pl.semaphore_wait(barrier, 3 * (SIDE - 1) + 1)
    t_begin(1)
    load_rest()
    for stage, at in ORDER:
        stages[stage](at)


def gathered(right_sides, leaf_bases, transfer, ranks, owners):
    dma, vmem = pltpu.SemaphoreType.DMA, pltpu.VMEM
    wide = (CHUNKS, RANK, WIDE)
    half = (CHUNKS, 2, HALF, WIDE)
    parts = (CHUNKS, SIDE, RANK, PART)
    scratch = [
        vmem((CHUNKS, SIDE, RANK, WIDE), F32),
        vmem((SIDE, RANK, RANK), BF16),
        vmem((SIDE, RANK, RANK), BF16),
        vmem((CHUNKS, SIDE, RANK, WIDE), BF16),
        vmem(half, BF16), vmem(half, BF16), vmem(half, BF16), vmem(half, BF16),
        vmem(wide, BF16), vmem(wide, BF16),
        vmem(parts, BF16), vmem(parts, BF16),
        vmem((CHUNKS, SIDE, 2, SIDE, QUARTER, PART), BF16),
        vmem((CHUNKS, SIDE, 2, SIDE, QUARTER, PART), BF16),
        vmem((CHUNKS, SIDE, PLANE, PIECE, PART), BF16),
        vmem((CHUNKS, 2 * BLOCKS, PIECE, PART), BF16),
        vmem((2 * BLOCKS, PIECE, PART), BF16),
        vmem((CHUNKS, BLOCKS, PIECE, PART), BF16),
        vmem((CHUNKS, SIDE, PLANE, PIECE, PART), BF16),
        vmem((CHUNKS, 2, 2, SIDE, QUARTER, PART), BF16),
        vmem((CHUNKS, 2, SIDE, RANK, PART), BF16),
        vmem(parts, BF16), vmem(parts, BF16),
        vmem((CHUNKS, 2, 2, RANK, PART), BF16), vmem((CHUNKS, SIDE, 2, RANK, PART), BF16),
        vmem(parts, BF16),
        vmem((LEVELS, SIDE, 2, RANK, RANK), BF16),
        vmem((2, RANK, RANK), BF16),
        vmem((1, 2 * BLOCKS), jnp.int32), pltpu.SMEM((1, 2 * BLOCKS), jnp.int32),
        dma((CHUNKS, SIDE)), dma(()), dma((LEVELS,)), dma(()), dma((LEVELS, 4)), dma((LEVELS, 4)),
        dma((CHUNKS, 6)), dma((CHUNKS, 6)), dma((CHUNKS, 3)), dma((CHUNKS, 3)),
        dma((CHUNKS, 6, SIDE)), dma((CHUNKS, 6, SIDE)), dma(()), dma(()),
        dma((CHUNKS, 6)), dma((CHUNKS, 7)),
    ]
    anywhere = pl.BlockSpec(memory_space=pl.ANY)
    in_vmem = pl.BlockSpec(memory_space=pltpu.VMEM)
    return pl.pallas_call(
        butterfly,
        out_shape=jax.ShapeDtypeStruct((SIDE, CHUNKS * SIDE, RANK, PART), BF16),
        in_specs=[anywhere, anywhere, anywhere, in_vmem, in_vmem],
        out_specs=anywhere,
        scratch_shapes=scratch,
        compiler_params=pltpu.CompilerParams(
            collective_id=0, has_side_effects=True, vmem_limit_bytes=58 * 1024 * 1024
        ),
        cost_estimate=pl.CostEstimate(
            flops=6 * 10**9, bytes_accessed=24 * 2**20, transcendentals=0
        ),
        name="butterfly",
    )(right_sides, leaf_bases, transfer, ranks, owners)


def expand_blocks(expand, skeleton, product, weights, tiles, done, in_sem, out_sem):
    loads = [
        (
            pltpu.make_async_copy(expand.at[j], weights.at[j], in_sem.at[j, 0]),
            pltpu.make_async_copy(skeleton.at[j], tiles.at[j], in_sem.at[j, 1]),
        )
        for j in range(SIDE)
    ]
    stores = [pltpu.make_async_copy(done.at[j], product.at[j], out_sem.at[j]) for j in range(SIDE)]
    for pair in loads:
        for copy in pair:
            copy.start()
    for j in range(SIDE):
        for copy in loads[j]:
            copy.wait()
        wide = jnp.concatenate([tiles[j, part] for part in range(CHUNKS * SIDE)], axis=1)
        done[j] = dot(weights[j], wide).astype(BF16)
        stores[j].start()
    for copy in stores:
        copy.wait()


def expanded(leaf_expand, skeleton):
    dma, vmem = pltpu.SemaphoreType.DMA, pltpu.VMEM
    anywhere = pl.BlockSpec(memory_space=pl.ANY)
    product = (SIDE, RANK, CHUNKS * WIDE)
    return pl.pallas_call(
        expand_blocks,
        out_shape=jax.ShapeDtypeStruct(product, BF16),
        in_specs=[anywhere, anywhere],
        out_specs=anywhere,
        scratch_shapes=[
            vmem(leaf_expand.shape, BF16), vmem(skeleton.shape, BF16), vmem(product, BF16),
            dma((SIDE, 2)), dma((SIDE,)),
        ],
        compiler_params=pltpu.CompilerParams(vmem_limit_bytes=58 * 1024 * 1024),
        name="expand",
    )(leaf_expand, skeleton)


def local(right_sides, leaf_bases, leaf_expand, transfer, skeleton_ranks, owner_map):
    skeleton = gathered(right_sides, leaf_bases, transfer, skeleton_ranks.T, owner_map[None, :])
    return expanded(leaf_expand, skeleton)


def solution(mesh):
    in_specs = (
        P("leaf", "rhs", None),
        P("leaf", "rhs", None),
        P("leaf", "rhs", None),
        P(None, "leaf", None, None, None),
        P(None, "leaf"),
        P(),
    )
    out_specs = P("leaf", "rhs", None)
    return jax.shard_map(local, mesh=mesh, in_specs=in_specs, out_specs=out_specs, check_vma=False)
```
